32 devices in a mesh: gz: 4 (over y, x), row: 2 (over core), col: 4 (over z).
Axes of the slice: x: 2, y: 2, z: 4, core: 2. Of those that a mesh axis runs over, the one named last changes fastest.
Arguments:
- leaf_probe: bfloat16 [32, 512, 128], P(('gz', 'row', 'col')), may hold values from -6 to 6
- leaf_lower_inv: bfloat16 [32, 512, 512], P(('gz', 'row', 'col')), may hold values from -0.25 to 0.25
- leaf_upper_inv: bfloat16 [32, 512, 512], P(('gz', 'row', 'col')), may hold values from -0.25 to 0.25
- leaf_lower_panel: bfloat16 [32, 1024, 512], P(('gz', 'row', 'col')), may hold values from -0.09375 to 0.09375
- leaf_upper_panel: bfloat16 [32, 512, 1024], P(('gz', 'row', 'col')), may hold values from -0.1875 to 0.1875
- leaf_tiles: int32 [32], P(('gz', 'row', 'col')), may hold values from 1 to 4, as said below
- coupled: int32 [32, 8], P(('gz', 'row', 'col')), may hold values from 0 to 31, as said below
- top_probe: bfloat16 [4, 1024, 128], P(None, ('row', 'col')), may hold values from -6 to 6
- top_lower_inv: bfloat16 [4, 1024, 1024], P(None, ('row', 'col')), may hold values from -0.1875 to 0.1875
- top_lower_blocks: bfloat16 [6, 1024, 1024], P(None, ('row', 'col')), may hold values from -0.125 to 0.125
- top_upper_inv: bfloat16 [4, 1024, 1024], P(None, ('row', 'col')), may hold values from -0.1875 to 0.1875
- top_upper_blocks: bfloat16 [6, 1024, 1024], P(None, ('row', 'col')), may hold values from -0.125 to 0.125
Outputs:
- leaf_solution: float32 [32, 512, 128], P(('gz', 'row', 'col'))
- top_solution: float32 [4, 1024, 128], P(None, ('row', 'col'))
The draws below stay inside these ranges and needn't reach their ends.
Inputs may be any that keep to these rules, and one draw needn't show every extreme that they name: `leaf_tiles`: some leaf has 4 blocks. `coupled`: the 8 numbers of one leaf are distinct.
All inputs are finite; a program needn't handle non-finite values.
Results may differ from the reference program's by a relative error of at most 0.02.
Values may be sent and summed in bfloat16 or wider, within the bound.
A program may use at most 128 MiB of HBM per device.

```python
import jax
import jax.numpy as jnp
from jax import lax

COLS = 128
TILE = 128
WL = 512
NCT = 8
LEVELS = 4
PAIRS = 6
LEAVES = 32
SEP = 1024
ANC_TILES = 32


def draw_leaf_tiles(key, part):
    first_key, second_key = jax.random.split(jax.random.fold_in(key, 11))
    drawn = jax.random.randint(first_key, (LEAVES,), 1, WL // TILE + 1)
    chosen = jax.random.randint(second_key, (), 0, LEAVES)
    return jnp.where(jnp.arange(LEAVES) == chosen, WL // TILE, drawn).astype(jnp.int32)


def draw_coupled(key, part):
    leaf_keys = jax.random.split(jax.random.fold_in(key, 23), LEAVES)

    def one_leaf(leaf_key):
        return jax.random.permutation(leaf_key, ANC_TILES)[:NCT]
    return jax.vmap(one_leaf)(leaf_keys).astype(jnp.int32)


def block_levels(stream_key, dims, cuts, low, top_value):
    def one(axis_at, blocks):
        steps = jax.random.uniform(jax.random.fold_in(jax.random.fold_in(stream_key, 6), axis_at), (blocks,), jnp.float32, low / len(cuts), top_value / len(cuts))
        return jnp.repeat(jnp.exp(steps), dims[axis_at] // blocks).reshape((-1,) + (1,) * (len(dims) - axis_at - 1))

    loudness = one(*cuts[0])
    for cut in cuts[1:]:
        loudness = loudness * one(*cut)
    return loudness


def bell_draw(key, dims, scale, most, shards=(), held_as=jnp.bfloat16):
    entries = scale * jax.random.normal(key, dims, jnp.float32)
    if shards:
        entries = entries * block_levels(key, dims, shards, -0.22, 0.18)
    return jnp.clip(entries, -most, most).astype(held_as)


def setup_inputs(seed: int = 0) -> dict:
    splits = jax.random.split(jax.random.key(seed), 13)
    leaf_probe = bell_draw(splits[0], (LEAVES, WL, COLS), 1.0, 6.0, ((0, 32),))
    leaf_lower_inv = bell_draw(splits[1], (LEAVES, WL, WL), WL ** -0.5, 0.25, ((0, 32),))
    leaf_upper_inv = bell_draw(splits[2], (LEAVES, WL, WL), WL ** -0.5, 0.25, ((0, 32),))
    leaf_lower_panel = bell_draw(splits[3], (LEAVES, NCT * TILE, WL), (WL * LEAVES * NCT // ANC_TILES) ** -0.5, 0.09375, ((0, 32),))
    leaf_upper_panel = bell_draw(splits[4], (LEAVES, WL, NCT * TILE), (NCT * TILE) ** -0.5, 0.1875, ((0, 32),))
    leaf_tiles = draw_leaf_tiles(jax.random.fold_in(splits[12], 71), 0)
    coupled = draw_coupled(jax.random.fold_in(splits[12], 71), 0)
    top_probe = bell_draw(splits[7], (LEVELS, SEP, COLS), 1.0, 6.0, ((1, 8),))
    top_lower_inv = bell_draw(splits[8], (LEVELS, SEP, SEP), SEP ** -0.5, 0.1875, ((1, 8),))
    top_lower_blocks = bell_draw(splits[9], (PAIRS, SEP, SEP), (2 * SEP) ** -0.5, 0.125, ((1, 8),))
    top_upper_inv = bell_draw(splits[10], (LEVELS, SEP, SEP), SEP ** -0.5, 0.1875, ((1, 8),))
    top_upper_blocks = bell_draw(splits[11], (PAIRS, SEP, SEP), (2 * SEP) ** -0.5, 0.125, ((1, 8),))
    return dict(leaf_probe=leaf_probe, leaf_lower_inv=leaf_lower_inv, leaf_upper_inv=leaf_upper_inv, leaf_lower_panel=leaf_lower_panel, leaf_upper_panel=leaf_upper_panel, leaf_tiles=leaf_tiles, coupled=coupled, top_probe=top_probe, top_lower_inv=top_lower_inv, top_lower_blocks=top_lower_blocks, top_upper_inv=top_upper_inv, top_upper_blocks=top_upper_blocks)


def pair_index(higher, lower):
    return higher * (higher - 1) // 2 + lower


def reference(leaf_probe, leaf_lower_inv, leaf_upper_inv, leaf_lower_panel, leaf_upper_panel, leaf_tiles, coupled, top_probe, top_lower_inv, top_lower_blocks, top_upper_inv, top_upper_blocks):
    row_index = jnp.arange(WL, dtype=jnp.int32)

    def forward_leaf(leaf_item):
        probe_part, inverse_part, panel_part, live_tiles = leaf_item
        live_mask = (row_index < live_tiles * TILE)[:, None]
        masked = jnp.where(live_mask, probe_part, jnp.zeros_like(probe_part))
        solved = jnp.where(live_mask, jnp.dot(inverse_part, masked, preferred_element_type=jnp.float32), 0.0).astype(jnp.bfloat16)
        return solved, jnp.dot(panel_part, solved, preferred_element_type=jnp.float32)

    leaf_forward, contribution = lax.map(forward_leaf, (leaf_probe, leaf_lower_inv, leaf_lower_panel, leaf_tiles))
    update = jnp.zeros((ANC_TILES, TILE, COLS), jnp.float32)
    update = update.at[coupled.reshape(-1)].add(contribution.reshape(-1, TILE, COLS))
    update = update.reshape(LEVELS, SEP, COLS)
    forward_levels = []
    for level in range(LEVELS):
        target = top_probe[level].astype(jnp.float32) - update[level]
        for other in range(level):
            target = target - jnp.dot(top_lower_blocks[pair_index(level, other)], forward_levels[other], preferred_element_type=jnp.float32)
        target = target.astype(jnp.bfloat16)
        forward_levels.append(jnp.dot(top_lower_inv[level], target, preferred_element_type=jnp.float32).astype(jnp.bfloat16))
    solutions = [None] * LEVELS
    rounded = [None] * LEVELS
    for level in range(LEVELS - 1, -1, -1):
        target = forward_levels[level].astype(jnp.float32)
        for other in range(LEVELS - 1, level, -1):
            target = target - jnp.dot(top_upper_blocks[pair_index(other, level)], rounded[other], preferred_element_type=jnp.float32)
        target = target.astype(jnp.bfloat16)
        solutions[level] = jnp.dot(top_upper_inv[level], target, preferred_element_type=jnp.float32)
        rounded[level] = solutions[level].astype(jnp.bfloat16)
    whole_top = jnp.stack(rounded).reshape(ANC_TILES, TILE, COLS)

    def backward_leaf(leaf_item):
        forward_part, inverse_part, panel_part, live_tiles, blocks = leaf_item
        live_mask = (row_index < live_tiles * TILE)[:, None]
        picked = whole_top[blocks].reshape(NCT * TILE, COLS)
        target = forward_part.astype(jnp.float32) - jnp.dot(panel_part, picked, preferred_element_type=jnp.float32)
        target = jnp.where(live_mask, target, 0.0).astype(jnp.bfloat16)
        return jnp.where(live_mask, jnp.dot(inverse_part, target, preferred_element_type=jnp.float32), 0.0)

    leaf_solution = lax.map(backward_leaf, (leaf_forward, leaf_upper_inv, leaf_upper_panel, leaf_tiles, coupled))
    return leaf_solution, jnp.stack(solutions)
```

```python
import functools

import jax
import jax.numpy as jnp
from jax import lax
from jax.experimental import pallas as pl
from jax.experimental.pallas import tpu as pltpu
from jax.sharding import PartitionSpec as P

TILE = 128
F32 = jnp.float32
BF16 = jnp.bfloat16


def pair_index(higher, lower):
    return higher * (higher - 1) // 2 + lower


def dot_t(left, right):
    return lax.dot_general(left, right, (((1,), (1,)), ((), ())), preferred_element_type=F32)


def kernel(
    sizes,
    tiles_ref,
    coupled_ref,
    leaf_probe_hbm,
    leaf_lower_inv_hbm,
    leaf_lower_panel_hbm,
    top_probe_hbm,
    top_lower_inv_hbm,
    top_lower_blocks_hbm,
    top_upper_inv_hbm,
    top_upper_blocks_hbm,
    leaf_upper_panel_hbm,
    leaf_upper_inv_hbm,
    leaf_out,
    top_out,
    leaf_probe,
    leaf_lower_inv,
    leaf_lower_panel,
    top_probe,
    top_lower_inv,
    top_lower_blocks,
    top_upper_inv,
    top_upper_blocks,
    leaf_upper_panel,
    leaf_upper_inv,
    solved_t,
    blocks_t,
    probe_t,
    upd,
    row_in,
    row_sum,
    gz_in,
    gz_sum,
    col_in,
    rings,
    whole,
    load_sem,
    row_sems,
    gz_sems,
    col_sems,
    gather_sems,
    whole_sems,
):
    levels, n_gz, n_row, n_col, part, couplings, leaf_width = sizes
    group = n_row * n_col
    g, r, c = lax.axis_index("gz"), lax.axis_index("row"), lax.axis_index("col")
    d = r * n_col + c
    forward_steps = 2 * levels - 1

    sources = [
        (leaf_probe_hbm, leaf_probe),
        (leaf_lower_inv_hbm, leaf_lower_inv),
        (leaf_lower_panel_hbm, leaf_lower_panel),
        (top_probe_hbm, top_probe),
        (top_lower_inv_hbm, top_lower_inv),
        (top_lower_blocks_hbm, top_lower_blocks),
        (top_upper_inv_hbm, top_upper_inv),
        (top_upper_blocks_hbm, top_upper_blocks),
        (leaf_upper_panel_hbm, leaf_upper_panel),
        (leaf_upper_inv_hbm, leaf_upper_inv),
    ]
    loads = [
        pltpu.make_async_copy(src, dst, load_sem.at[i]) for i, (src, dst) in enumerate(sources)
    ]
    for load in loads:
        load.start()

    def each(count, step):
        lax.fori_loop(1, count, lambda i, carry: (step(i), carry)[1], 0, unroll=count <= 8)

    barrier = pltpu.get_barrier_semaphore()

    def group_peer(i):
        peer = lax.rem(d + i, group)
        return (g, lax.div(peer, n_col), lax.rem(peer, n_col))

    def gz_peer(i):
        return (lax.rem(g + i, n_gz), r, c)

    def greet(device):
        pl.semaphore_signal(barrier, inc=1, device_id=device, device_id_type=pl.DeviceIdType.MESH)

    each(group, lambda i: greet(group_peer(i)))
    each(n_gz, lambda i: greet(gz_peer(i)))

    def send(src, dst, sems, at, device):
        pltpu.make_async_remote_copy(
            src_ref=src,
            dst_ref=dst,
            send_sem=sems.at[0, at],
            recv_sem=sems.at[1, at],
            device_id=device,
            device_id_type=pl.DeviceIdType.MESH,
        ).start()

    def wait_bytes(ref, sem):
        pltpu.make_async_copy(ref, ref, sem).wait()

    def row_send(a):
        def step(i):
            other = lax.rem(r + i, n_row)
            send(upd.at[a, other], row_in.at[a, r], row_sems, a, (g, other, c))

        each(n_row, step)

    def row_finish(a):
        if n_row > 1:
            wait_bytes(row_in.at[a, pl.ds(0, n_row - 1)], row_sems.at[1, a])
        total = upd[a, r].astype(F32)
        for i in range(1, n_row):
            total = total + row_in[a, lax.rem(r + i, n_row)].astype(F32)
        row_sum[a] = total.astype(BF16)

    def gz_send(a):
        def step(i):
            other = lax.rem(g + i, n_gz)
            send(row_sum.at[a, other], gz_in.at[a, g], gz_sems, a, (other, r, c))

        each(n_gz, step)

    def gz_finish(a):
        if n_gz > 1:
            wait_bytes(gz_in.at[a, pl.ds(0, n_gz - 1)], gz_sems.at[1, a])
        total = row_sum[a, g].astype(F32)
        for i in range(1, n_gz):
            total = total + gz_in[a, lax.rem(g + i, n_gz)].astype(F32)
        gz_sum[a] = total.astype(BF16)

    def col_send(a):
        def step(i):
            other = lax.rem(c + i, n_col)
            send(gz_sum.at[a, other], col_in.at[a, c], col_sems, a, (g, r, other))

        each(n_col, step)

    def col_finish(a):
        if n_col > 1:
            wait_bytes(col_in.at[a, pl.ds(0, n_col - 1)], col_sems.at[1, a])
        total = gz_sum[a, c].astype(F32)
        for i in range(1, n_col):
            total = total + col_in[a, lax.rem(c + i, n_col)].astype(F32)
        return probe_t[a, g] - total

    def gather_send(step_at, value):
        rings[step_at, d] = value

        def step(i):
            send(rings.at[step_at, d], rings.at[step_at, d], gather_sems, step_at, group_peer(i))

        each(group, step)

    def gather_wait(step_at):
        if group > 1:
            wait_bytes(rings.at[step_at, pl.ds(0, group - 1)], gather_sems.at[1, step_at])
        return jnp.concatenate([rings[step_at, i] for i in range(group)], axis=1)

    def solved_send(a, value):
        at = a * group + d
        whole[g, at] = value

        def step(i):
            send(whole.at[g, at], whole.at[g, at], gather_sems, 3 * levels - 1 + a, group_peer(i))

        each(group, step)

    def solved_wait(a):
        if group > 1:
            wait_bytes(
                whole.at[g, pl.ds(a * group, group - 1)], gather_sems.at[1, 3 * levels - 1 + a]
            )
        return jnp.concatenate([whole[g, a * group + i] for i in range(group)], axis=1)

    def whole_send(a):
        def step(i):
            at = pl.ds(a * group, group)
            send(whole.at[g, at], whole.at[g, at], whole_sems, a, gz_peer(i))

        each(n_gz, step)

    def whole_wait(a):
        if n_gz > 1:
            wait_bytes(whole.at[pl.ds(0, n_gz - 1), pl.ds(a * group, group)], whole_sems.at[1, a])

    live = lax.broadcasted_iota(jnp.int32, (1, leaf_width), 1) < tiles_ref[0] * TILE
    loads[0].wait()
    masked = jnp.where(live, leaf_probe[0].astype(F32).T, 0.0).astype(BF16)
    loads[1].wait()
    solved = jnp.where(live, dot_t(masked, leaf_lower_inv[0]), 0.0).astype(BF16)
    solved_t[...] = solved
    loads[2].wait()
    for j in range(couplings):
        rows = leaf_lower_panel[0, pl.ds(j * TILE, TILE), :]
        blocks_t[j] = dot_t(solved, rows).astype(BF16)
    blocks_t[couplings] = jnp.zeros(blocks_t.shape[1:], BF16)

    def spread(a):
        def place(t, carry):
            at = jnp.int32(couplings)
            for j in range(couplings):
                at = jnp.where(coupled_ref[0, j] == a * group + t, j, at)
            block = blocks_t[at]
            t_row, t_col = lax.div(t, n_col), lax.rem(t, n_col)
            for k in range(n_gz):
                upd[a, t_row, k, t_col] = block[k * part : (k + 1) * part]
            return carry

        lax.fori_loop(0, group, place, 0)

    spread(0)
    pl.semaphore_wait(barrier, group - 1 + n_gz - 1)
    row_send(0)
    for a in range(1, levels):
        spread(a)
        row_send(a)
    row_finish(0)
    gz_send(0)
    loads[3].wait()
    for a in range(levels):
        probe_t[a] = top_probe[a].astype(F32).T.reshape(probe_t.shape[1:])
    for a in range(1, levels):
        row_finish(a)
        gz_send(a)
    gz_finish(0)
    col_send(0)
    loads[4].wait()
    loads[5].wait()
    target = {0: col_finish(0)}

    forward = []
    for a in range(levels):
        gather_send(2 * a, target[a].astype(BF16))
        if a + 1 < levels:
            gz_finish(a + 1)
            col_send(a + 1)
        if a >= 1:
            for h in range(a + 1, levels):
                known = [l for l in range(levels) if l == a - 1]
                for l in known:
                    pending[h] = pending.get(h, 0.0) + dot_t(gathered[l], top_lower_blocks[pair_index(h, l)])
        else:
            gathered = []
            pending = {}
        whole_rhs = gather_wait(2 * a)
        x = dot_t(whole_rhs, top_lower_inv[a]).astype(BF16)
        forward.append(x)
        if a + 1 < levels:
            gather_send(2 * a + 1, x)
            base = col_finish(a + 1) - pending.get(a + 1, 0.0)
            if a == 0:
                loads[6].wait()
                loads[7].wait()
            gathered.append(gather_wait(2 * a + 1))
            target[a + 1] = base - dot_t(gathered[a], top_lower_blocks[pair_index(a + 1, a)])

    rhs = forward[levels - 1]
    upper = {a: forward[a].astype(F32) for a in range(levels)}
    last = None
    for a in range(levels - 1, -1, -1):
        gather_send(forward_steps + a, rhs)
        if last is not None:
            whole_send(a + 1)
            for l in range(a):
                upper[l] = upper[l] - dot_t(last, top_upper_blocks[pair_index(a + 1, l)])
        whole_rhs = gather_wait(forward_steps + a)
        solution_part = dot_t(whole_rhs, top_upper_inv[a]).astype(BF16)
        solved_send(a, solution_part)
        if a == levels - 1:
            loads[8].wait()
            loads[9].wait()
        last = solved_wait(a)
        if a > 0:
            rhs = (upper[a - 1] - dot_t(last, top_upper_blocks[pair_index(a, a - 1)])).astype(BF16)
    whole_send(0)

    def write_top(a):
        whole_wait(a)
        own = jnp.concatenate([whole[k, a * group + d] for k in range(n_gz)], axis=0)
        top_out[a] = own.astype(F32).T

    for a in range(levels - 1, 0, -1):
        write_top(a)
    whole_wait(0)
    picked = jnp.concatenate(
        [
            jnp.concatenate([whole[k, coupled_ref[0, j]] for k in range(n_gz)], axis=0)
            for j in range(couplings)
        ],
        axis=1,
    )
    back = solved_t[...].astype(F32) - dot_t(picked, leaf_upper_panel[0])
    back = jnp.where(live, back, 0.0).astype(BF16)
    answer = dot_t(leaf_upper_inv[0], back)
    live_rows = lax.broadcasted_iota(jnp.int32, (leaf_width, 1), 0) < tiles_ref[0] * TILE
    leaf_out[0] = jnp.where(live_rows, answer, 0.0)
    own = jnp.concatenate([whole[k, d] for k in range(n_gz)], axis=0)
    top_out[0] = own.astype(F32).T

    for a in range(levels):
        if n_row > 1:
            wait_bytes(row_in.at[a, pl.ds(0, n_row - 1)], row_sems.at[0, a])
        if n_gz > 1:
            wait_bytes(gz_in.at[a, pl.ds(0, n_gz - 1)], gz_sems.at[0, a])
            wait_bytes(whole.at[pl.ds(0, n_gz - 1), pl.ds(a * group, group)], whole_sems.at[0, a])
        if n_col > 1:
            wait_bytes(col_in.at[a, pl.ds(0, n_col - 1)], col_sems.at[0, a])
    if group > 1:
        for s in range(4 * levels - 1):
            wait_bytes(rings.at[0, pl.ds(0, group - 1)], gather_sems.at[0, s])


def solution(mesh):
    n_gz, n_row, n_col = mesh.shape["gz"], mesh.shape["row"], mesh.shape["col"]
    group = n_row * n_col

    def body(
        leaf_probe,
        leaf_lower_inv,
        leaf_upper_inv,
        leaf_lower_panel,
        leaf_upper_panel,
        leaf_tiles,
        coupled,
        top_probe,
        top_lower_inv,
        top_lower_blocks,
        top_upper_inv,
        top_upper_blocks,
    ):
        leaves, leaf_width, columns = leaf_probe.shape
        levels, sep_rows, _ = top_probe.shape
        couplings = coupled.shape[1]
        part = columns // n_gz
        assert leaves == 1 and sep_rows == TILE and part * n_gz == columns
        big = [
            leaf_probe,
            leaf_lower_inv,
            leaf_lower_panel,
            top_probe,
            top_lower_inv,
            top_lower_blocks,
            top_upper_inv,
            top_upper_blocks,
            leaf_upper_panel,
            leaf_upper_inv,
        ]
        sizes = (levels, n_gz, n_row, n_col, part, couplings, leaf_width)
        dma = pltpu.SemaphoreType.DMA
        smem = pl.BlockSpec(memory_space=pltpu.SMEM)
        vmem = pl.BlockSpec(memory_space=pltpu.VMEM)
        anywhere = pl.BlockSpec(memory_space=pl.ANY)
        scratch = [pltpu.VMEM(x.shape, x.dtype) for x in big] + [
            pltpu.VMEM((columns, leaf_width), BF16),
            pltpu.VMEM((couplings + 1, columns, TILE), BF16),
            pltpu.VMEM((levels, n_gz, part, TILE), F32),
            pltpu.VMEM((levels, n_row, n_gz, n_col, part, TILE), BF16),
            pltpu.VMEM((levels, n_row, n_gz, n_col, part, TILE), BF16),
            pltpu.VMEM((levels, n_gz, n_col, part, TILE), BF16),
            pltpu.VMEM((levels, n_gz, n_col, part, TILE), BF16),
            pltpu.VMEM((levels, n_col, part, TILE), BF16),
            pltpu.VMEM((levels, n_col, part, TILE), BF16),
            pltpu.VMEM((3 * levels - 1, group, part, TILE), BF16),
            pltpu.VMEM((n_gz, levels * group, part, TILE), BF16),
            dma((len(big),)),
            dma((2, levels)),
            dma((2, levels)),
            dma((2, levels)),
            dma((2, 4 * levels - 1)),
            dma((2, levels)),
        ]
        return pl.pallas_call(
            functools.partial(kernel, sizes),
            out_shape=(
                jax.ShapeDtypeStruct(leaf_probe.shape, F32),
                jax.ShapeDtypeStruct(top_probe.shape, F32),
            ),
            in_specs=[smem, smem] + [anywhere] * len(big),
            out_specs=(vmem, vmem),
            scratch_shapes=scratch,
            compiler_params=pltpu.CompilerParams(
                collective_id=0, has_side_effects=True, vmem_limit_bytes=56 * 2**20
            ),
        )(leaf_tiles, coupled, *big)

    leaf3 = P(("gz", "row", "col"), None, None)
    top3 = P(None, ("row", "col"), None)
    return jax.shard_map(
        body,
        mesh=mesh,
        in_specs=(
            leaf3,
            leaf3,
            leaf3,
            leaf3,
            leaf3,
            P(("gz", "row", "col")),
            P(("gz", "row", "col"), None),
            top3,
            top3,
            top3,
            top3,
            top3,
        ),
        out_specs=(leaf3, top3),
        check_vma=False,
    )
```

```python
import functools

import jax
import jax.numpy as jnp
from jax import lax
from jax.experimental import pallas as pl
from jax.experimental.pallas import tpu as pltpu
from jax.sharding import PartitionSpec as P

TILE = 128
F32 = jnp.float32
BF16 = jnp.bfloat16


def pair_index(higher, lower):
    return higher * (higher - 1) // 2 + lower


def dot_t(left, right):
    return lax.dot_general(left, right, (((1,), (1,)), ((), ())), preferred_element_type=F32)


def kernel(
    sizes,
    tiles_ref,
    coupled_ref,
    leaf_probe_hbm,
    leaf_lower_inv_hbm,
    leaf_lower_panel_hbm,
    top_probe_hbm,
    top_lower_inv_hbm,
    top_lower_blocks_hbm,
    top_upper_inv_hbm,
    top_upper_blocks_hbm,
    leaf_upper_panel_hbm,
    leaf_upper_inv_hbm,
    leaf_out,
    top_out,
    leaf_probe,
    leaf_lower_inv,
    leaf_lower_panel,
    top_probe,
    top_lower_inv,
    top_lower_blocks,
    top_upper_inv,
    top_upper_blocks,
    leaf_upper_panel,
    leaf_upper_inv,
    solved_t,
    blocks_t,
    probe_t,
    upd,
    row_in,
    row_sum,
    gz_in,
    gz_sum,
    col_in,
    rings,
    whole,
    load_sem,
    pair_sems,
    row_sems,
    gz_sems,
    col_sems,
    gather_sems,
    whole_sems,
):
    levels, n_gz, n_row, n_col, pair, part, couplings, leaf_width = sizes
    group = n_row * n_col
    teams, parts = group // pair, n_gz * pair
    g, r, c = lax.axis_index("gz"), lax.axis_index("row"), lax.axis_index("col")
    d = r * n_col + c
    base_row, q = lax.div(r, pair) * pair, lax.rem(r, pair)
    team = lax.div(r, pair) * n_col + c
    piece = g * pair + q
    forward_steps = 2 * levels - 1

    sources = [
        (leaf_probe_hbm, leaf_probe),
        (leaf_lower_inv_hbm, leaf_lower_inv),
        (leaf_lower_panel_hbm, leaf_lower_panel),
        (top_probe_hbm, top_probe),
        (top_lower_inv_hbm, top_lower_inv),
        (top_lower_blocks_hbm, top_lower_blocks),
        (top_upper_inv_hbm, top_upper_inv),
        (top_upper_blocks_hbm, top_upper_blocks),
        (leaf_upper_panel_hbm, leaf_upper_panel),
        (leaf_upper_inv_hbm, leaf_upper_inv),
    ]
    shared = range(3, 8)
    loads = [
        pltpu.make_async_copy(src, dst.at[:, q] if i in shared else dst, load_sem.at[i])
        for i, (src, dst) in enumerate(sources)
    ]
    for load in loads:
        load.start()

    def each(count, step):
        lax.fori_loop(1, count, lambda i, carry: (step(i), carry)[1], 0, unroll=count <= 8)

    barrier = pltpu.get_barrier_semaphore()

    def group_peer(i):
        peer = lax.rem(d + i, group)
        return (g, lax.div(peer, n_col), lax.rem(peer, n_col))

    def gz_peer(i):
        return (lax.rem(g + i, n_gz), r, c)

    def team_peer(i):
        peer = lax.rem(team + i, teams)
        return (g, lax.div(peer, n_col) * pair + q, lax.rem(peer, n_col))

    def piece_peer(i):
        peer = lax.rem(piece + i, parts)
        return (lax.div(peer, pair), base_row + lax.rem(peer, pair), c)

    def far_peer(i):
        at = i - 1
        layer = lax.rem(g + 1 + lax.div(at, pair), n_gz)
        return (layer, base_row + lax.rem(at, pair), c)

    def greet(device):
        pl.semaphore_signal(barrier, inc=1, device_id=device, device_id_type=pl.DeviceIdType.MESH)

    each(group, lambda i: greet(group_peer(i)))
    each((n_gz - 1) * pair + 1, lambda i: greet(far_peer(i)))

    def send(src, dst, sems, at, device):
        pltpu.make_async_remote_copy(
            src_ref=src,
            dst_ref=dst,
            send_sem=sems.at[0, at],
            recv_sem=sems.at[1, at],
            device_id=device,
            device_id_type=pl.DeviceIdType.MESH,
        ).start()

    def wait_bytes(ref, sem):
        pltpu.make_async_copy(ref, ref, sem).wait()

    def pair_send(w):
        src, dst = sources[w]

        def step(i):
            to = (g, base_row + lax.rem(q + i, pair), c)
            send(src, dst.at[:, q], pair_sems, w - shared[0], to)

        each(pair, step)

    def ready(w):
        loads[w].wait()
        if pair > 1:
            ref = sources[w][1]
            wait_bytes(ref.at[:, pl.ds(0, pair - 1)], pair_sems.at[1, w - shared[0]])

    def weight(ref, at):
        return ref[at].reshape(pair * TILE, ref.shape[-1])

    def side_by_side(value):
        return jnp.concatenate([value[k] for k in range(pair)], axis=1)

    def in_order(block):
        order = [(t // n_col, t % n_col) for t in range(group)]
        return jnp.concatenate([block(x // pair * n_col + y, x % pair) for x, y in order], axis=1)

    def row_send(a):
        def step(i):
            other = lax.rem(r + i, n_row)
            send(upd.at[a, other], row_in.at[a, r], row_sems, a, (g, other, c))

        each(n_row, step)

    def row_finish(a):
        if n_row > 1:
            wait_bytes(row_in.at[a, pl.ds(0, n_row - 1)], row_sems.at[1, a])
        total = upd[a, r].astype(F32)
        for i in range(1, n_row):
            total = total + row_in[a, lax.rem(r + i, n_row)].astype(F32)
        row_sum[a] = total.astype(BF16)

    def gz_send(a):
        def step(i):
            other = lax.rem(g + i, n_gz)
            send(row_sum.at[a, other], gz_in.at[a, g], gz_sems, a, (other, r, c))

        each(n_gz, step)

    def gz_finish(a):
        if n_gz > 1:
            wait_bytes(gz_in.at[a, pl.ds(0, n_gz - 1)], gz_sems.at[1, a])
        total = row_sum[a, g].astype(F32)
        for i in range(1, n_gz):
            total = total + gz_in[a, lax.rem(g + i, n_gz)].astype(F32)
        gz_sum[a] = total.astype(BF16)

    def col_send(a):
        def step(i):
            other = lax.rem(c + i, n_col)
            send(gz_sum.at[a, other], col_in.at[a, c], col_sems, a, (g, r, other))

        each(n_col, step)

    def col_finish(a):
        if n_col > 1:
            wait_bytes(col_in.at[a, pl.ds(0, n_col - 1)], col_sems.at[1, a])
        total = gz_sum[a, c].astype(F32)
        for i in range(1, n_col):
            total = total + col_in[a, lax.rem(c + i, n_col)].astype(F32)
        return side_by_side(probe_t[a, :, piece] - total)

    def gather_send(step_at, value):
        for k in range(pair):
            rings[step_at, team, k] = value[:, k * TILE : (k + 1) * TILE]

        def step(i):
            own = rings.at[step_at, team]
            send(own, own, gather_sems, step_at, team_peer(i))

        each(teams, step)

    def gather_wait(step_at):
        if teams > 1:
            wait_bytes(rings.at[step_at, pl.ds(0, teams - 1)], gather_sems.at[1, step_at])
        return in_order(lambda at, k: rings[step_at, at, k])

    def solved_send(a, value):
        at = a * teams + team
        for k in range(pair):
            whole[piece, at, k] = value[:, k * TILE : (k + 1) * TILE]

        def step(i):
            own = whole.at[piece, at]
            send(own, own, gather_sems, 3 * levels - 1 + a, team_peer(i))

        each(teams, step)

    def solved_wait(a):
        if teams > 1:
            wait_bytes(
                whole.at[piece, pl.ds(a * teams, teams - 1)], gather_sems.at[1, 3 * levels - 1 + a]
            )
        return in_order(lambda at, k: whole[piece, a * teams + at, k])

    def whole_send(a):
        def step(i):
            own = whole.at[piece, pl.ds(a * teams, teams)]
            send(own, own, whole_sems, a, piece_peer(i))

        each(parts, step)

    def whole_wait(a):
        if parts > 1:
            wait_bytes(whole.at[pl.ds(0, parts - 1), pl.ds(a * teams, teams)], whole_sems.at[1, a])

    live = lax.broadcasted_iota(jnp.int32, (1, leaf_width), 1) < tiles_ref[0] * TILE
    loads[0].wait()
    masked = jnp.where(live, leaf_probe[0].astype(F32).T, 0.0).astype(BF16)
    loads[1].wait()
    solved = jnp.where(live, dot_t(masked, leaf_lower_inv[0]), 0.0).astype(BF16)
    solved_t[...] = solved
    pl.semaphore_wait(barrier, group - 1 + (n_gz - 1) * pair)
    for w in (3, 4, 5):
        pair_send(w)
    loads[2].wait()
    for j in range(couplings):
        rows = leaf_lower_panel[0, pl.ds(j * TILE, TILE), :]
        blocks_t[j] = dot_t(solved, rows).astype(BF16)
    blocks_t[couplings] = jnp.zeros(blocks_t.shape[1:], BF16)

    def spread(a):
        def place(t, carry):
            at = jnp.int32(couplings)
            for j in range(couplings):
                at = jnp.where(coupled_ref[0, j] == a * group + t, j, at)
            block = blocks_t[at]
            t_row, t_col = lax.div(t, n_col), lax.rem(t, n_col)
            first, place_in = lax.div(t_row, pair) * pair, lax.rem(t_row, pair)
            for k in range(parts):
                lines = block[k * part : (k + 1) * part]
                upd[a, first + k % pair, k // pair, t_col, place_in] = lines
            return carry

        lax.fori_loop(0, group, place, 0)

    spread(0)
    row_send(0)
    for a in range(1, levels):
        spread(a)
        row_send(a)
    row_finish(0)
    gz_send(0)
    ready(3)
    for a in range(levels):
        for k in range(pair):
            probe_t[a, k] = top_probe[a, k].astype(F32).T.reshape(probe_t.shape[2:])
    for a in range(1, levels):
        row_finish(a)
        gz_send(a)
    gz_finish(0)
    col_send(0)
    for w in (6, 7):
        pair_send(w)
    ready(4)
    ready(5)
    target = {0: col_finish(0)}

    forward = []
    for a in range(levels):
        gather_send(2 * a, target[a].astype(BF16))
        if a + 1 < levels:
            gz_finish(a + 1)
            col_send(a + 1)
        if a >= 1:
            for h in range(a + 1, levels):
                known = [l for l in range(levels) if l == a - 1]
                for l in known:
                    pending[h] = pending.get(h, 0.0) + dot_t(gathered[l], weight(top_lower_blocks, pair_index(h, l)))
        else:
            gathered = []
            pending = {}
        whole_rhs = gather_wait(2 * a)
        x = dot_t(whole_rhs, weight(top_lower_inv, a)).astype(BF16)
        forward.append(x)
        if a + 1 < levels:
            gather_send(2 * a + 1, x)
            base = col_finish(a + 1) - pending.get(a + 1, 0.0)
            gathered.append(gather_wait(2 * a + 1))
            target[a + 1] = base - dot_t(gathered[a], weight(top_lower_blocks, pair_index(a + 1, a)))

    ready(6)
    ready(7)
    rhs = forward[levels - 1]
    upper = {a: forward[a].astype(F32) for a in range(levels)}
    last = None
    for a in range(levels - 1, -1, -1):
        gather_send(forward_steps + a, rhs)
        if last is not None:
            whole_send(a + 1)
            for l in range(a):
                upper[l] = upper[l] - dot_t(last, weight(top_upper_blocks, pair_index(a + 1, l)))
        whole_rhs = gather_wait(forward_steps + a)
        solution_part = dot_t(whole_rhs, weight(top_upper_inv, a)).astype(BF16)
        solved_send(a, solution_part)
        if a == levels - 1:
            loads[8].wait()
            loads[9].wait()
        last = solved_wait(a)
        if a > 0:
            rhs = (upper[a - 1] - dot_t(last, weight(top_upper_blocks, pair_index(a, a - 1)))).astype(BF16)
    whole_send(0)

    def write_top(a):
        whole_wait(a)
        own = jnp.concatenate([whole[k, a * teams + team, q] for k in range(parts)], axis=0)
        top_out[a] = own.astype(F32).T

    for a in range(levels - 1, 0, -1):
        write_top(a)
    whole_wait(0)

    def where(tile):
        level, t = lax.div(tile, group), lax.rem(tile, group)
        x, y = lax.div(t, n_col), lax.rem(t, n_col)
        return level * teams + lax.div(x, pair) * n_col + y, lax.rem(x, pair)

    picked = jnp.concatenate(
        [
            jnp.concatenate([whole[(k, *where(coupled_ref[0, j]))] for k in range(parts)], axis=0)
            for j in range(couplings)
        ],
        axis=1,
    )
    back = solved_t[...].astype(F32) - dot_t(picked, leaf_upper_panel[0])
    back = jnp.where(live, back, 0.0).astype(BF16)
    answer = dot_t(leaf_upper_inv[0], back)
    live_rows = lax.broadcasted_iota(jnp.int32, (leaf_width, 1), 0) < tiles_ref[0] * TILE
    leaf_out[0] = jnp.where(live_rows, answer, 0.0)
    own = jnp.concatenate([whole[k, team, q] for k in range(parts)], axis=0)
    top_out[0] = own.astype(F32).T

    for a in range(levels):
        if n_row > 1:
            wait_bytes(row_in.at[a, pl.ds(0, n_row - 1)], row_sems.at[0, a])
        if n_gz > 1:
            wait_bytes(gz_in.at[a, pl.ds(0, n_gz - 1)], gz_sems.at[0, a])
        if parts > 1:
            wait_bytes(whole.at[pl.ds(0, parts - 1), pl.ds(a * teams, teams)], whole_sems.at[0, a])
        if n_col > 1:
            wait_bytes(col_in.at[a, pl.ds(0, n_col - 1)], col_sems.at[0, a])
    if teams > 1:
        for s in range(4 * levels - 1):
            wait_bytes(rings.at[0, pl.ds(0, teams - 1)], gather_sems.at[0, s])
    if pair > 1:
        for w in shared:
            ref = sources[w][1]
            wait_bytes(ref.at[:, pl.ds(0, pair - 1)], pair_sems.at[0, w - shared[0]])


def solution(mesh):
    n_gz, n_row, n_col = mesh.shape["gz"], mesh.shape["row"], mesh.shape["col"]
    group = n_row * n_col

    def body(
        leaf_probe,
        leaf_lower_inv,
        leaf_upper_inv,
        leaf_lower_panel,
        leaf_upper_panel,
        leaf_tiles,
        coupled,
        top_probe,
        top_lower_inv,
        top_lower_blocks,
        top_upper_inv,
        top_upper_blocks,
    ):
        leaves, leaf_width, columns = leaf_probe.shape
        levels, sep_rows, _ = top_probe.shape
        couplings = coupled.shape[1]
        weights = (top_lower_inv, top_lower_blocks, top_upper_inv, top_upper_blocks)
        small = sum(x.size * x.dtype.itemsize for x in weights) <= 12 * 2**20
        pair = 2 if small and n_row % 2 == 0 and columns % (n_gz * 32) == 0 else 1
        teams, parts = group // pair, n_gz * pair
        part = columns // parts
        assert leaves == 1 and sep_rows == TILE and part * parts == columns
        big = [
            leaf_probe,
            leaf_lower_inv,
            leaf_lower_panel,
            top_probe,
            top_lower_inv,
            top_lower_blocks,
            top_upper_inv,
            top_upper_blocks,
            leaf_upper_panel,
            leaf_upper_inv,
        ]
        sizes = (levels, n_gz, n_row, n_col, pair, part, couplings, leaf_width)
        dma = pltpu.SemaphoreType.DMA
        smem = pl.BlockSpec(memory_space=pltpu.SMEM)
        vmem = pl.BlockSpec(memory_space=pltpu.VMEM)
        anywhere = pl.BlockSpec(memory_space=pl.ANY)
        held = [
            (x.shape[0], pair, *x.shape[1:]) if i in range(3, 8) else x.shape
            for i, x in enumerate(big)
        ]
        scratch = [pltpu.VMEM(shape, x.dtype) for shape, x in zip(held, big)] + [
            pltpu.VMEM((columns, leaf_width), BF16),
            pltpu.VMEM((couplings + 1, columns, TILE), BF16),
            pltpu.VMEM((levels, pair, parts, part, TILE), F32),
            pltpu.VMEM((levels, n_row, n_gz, n_col, pair, part, TILE), BF16),
            pltpu.VMEM((levels, n_row, n_gz, n_col, pair, part, TILE), BF16),
            pltpu.VMEM((levels, n_gz, n_col, pair, part, TILE), BF16),
            pltpu.VMEM((levels, n_gz, n_col, pair, part, TILE), BF16),
            pltpu.VMEM((levels, n_col, pair, part, TILE), BF16),
            pltpu.VMEM((levels, n_col, pair, part, TILE), BF16),
            pltpu.VMEM((3 * levels - 1, teams, pair, part, TILE), BF16),
            pltpu.VMEM((parts, levels * teams, pair, part, TILE), BF16),
            dma((len(big),)),
            dma((2, 5)),
            dma((2, levels)),
            dma((2, levels)),
            dma((2, levels)),
            dma((2, 4 * levels - 1)),
            dma((2, levels)),
        ]
        return pl.pallas_call(
            functools.partial(kernel, sizes),
            out_shape=(
                jax.ShapeDtypeStruct(leaf_probe.shape, F32),
                jax.ShapeDtypeStruct(top_probe.shape, F32),
            ),
            in_specs=[smem, smem] + [anywhere] * len(big),
            out_specs=(vmem, vmem),
            scratch_shapes=scratch,
            compiler_params=pltpu.CompilerParams(
                collective_id=0, has_side_effects=True, vmem_limit_bytes=56 * 2**20
            ),
        )(leaf_tiles, coupled, *big)

    leaf3 = P(("gz", "row", "col"), None, None)
    top3 = P(None, ("row", "col"), None)
    return jax.shard_map(
        body,
        mesh=mesh,
        in_specs=(
            leaf3,
            leaf3,
            leaf3,
            leaf3,
            leaf3,
            P(("gz", "row", "col")),
            P(("gz", "row", "col"), None),
            top3,
            top3,
            top3,
            top3,
            top3,
        ),
        out_specs=(leaf3, top3),
        check_vma=False,
    )
```

```python
import functools

import jax
import jax.numpy as jnp
from jax import lax
from jax.experimental import pallas as pl
from jax.experimental.pallas import tpu as pltpu
from jax.sharding import PartitionSpec as P

TILE = 128
F32 = jnp.float32
BF16 = jnp.bfloat16


def pair_index(higher, lower):
    return higher * (higher - 1) // 2 + lower


def dot_t(left, right):
    return lax.dot_general(left, right, (((1,), (1,)), ((), ())), preferred_element_type=F32)


def dot_few(few, matrix):
    return dot_t(matrix, few).T


def kernel(
    sizes,
    tiles_ref,
    coupled_ref,
    leaf_probe_hbm,
    leaf_lower_inv_hbm,
    leaf_lower_panel_hbm,
    top_probe_hbm,
    top_lower_inv_hbm,
    top_lower_blocks_hbm,
    top_upper_inv_hbm,
    top_upper_blocks_hbm,
    leaf_upper_panel_hbm,
    leaf_upper_inv_hbm,
    leaf_out,
    top_out,
    leaf_probe,
    leaf_lower_inv,
    leaf_lower_panel,
    top_probe,
    top_lower_inv,
    top_lower_blocks,
    top_upper_inv,
    top_upper_blocks,
    leaf_upper_panel,
    leaf_upper_inv,
    solved_t,
    blocks_t,
    probe_t,
    upd,
    row_in,
    row_sum,
    gz_in,
    gz_sum,
    col_in,
    rings,
    whole,
    load_sem,
    pair_sems,
    row_sems,
    gz_sems,
    col_sems,
    gather_sems,
    whole_sems,
):
    levels, n_gz, n_row, n_col, pair, part, couplings, leaf_width = sizes
    group = n_row * n_col
    teams, parts = group // pair, n_gz * pair
    g, r, c = lax.axis_index("gz"), lax.axis_index("row"), lax.axis_index("col")
    d = r * n_col + c
    base_row, q = lax.div(r, pair) * pair, lax.rem(r, pair)
    team = lax.div(r, pair) * n_col + c
    piece = g * pair + q
    forward_steps = 2 * levels - 1

    sources = [
        (leaf_probe_hbm, leaf_probe),
        (leaf_lower_inv_hbm, leaf_lower_inv),
        (leaf_lower_panel_hbm, leaf_lower_panel),
        (top_probe_hbm, top_probe),
        (top_lower_inv_hbm, top_lower_inv),
        (top_lower_blocks_hbm, top_lower_blocks),
        (top_upper_inv_hbm, top_upper_inv),
        (top_upper_blocks_hbm, top_upper_blocks),
        (leaf_upper_panel_hbm, leaf_upper_panel),
        (leaf_upper_inv_hbm, leaf_upper_inv),
    ]
    shared = range(3, 8)
    loads = [
        pltpu.make_async_copy(src, dst.at[:, q] if i in shared else dst, load_sem.at[i])
        for i, (src, dst) in enumerate(sources)
    ]
    for load in loads:
        load.start()

    def each(count, step):
        lax.fori_loop(1, count, lambda i, carry: (step(i), carry)[1], 0, unroll=count <= 8)

    barrier = pltpu.get_barrier_semaphore()

    def group_peer(i):
        peer = lax.rem(d + i, group)
        return (g, lax.div(peer, n_col), lax.rem(peer, n_col))

    def gz_peer(i):
        return (lax.rem(g + i, n_gz), r, c)

    def team_peer(i):
        peer = lax.rem(team + i, teams)
        return (g, lax.div(peer, n_col) * pair + q, lax.rem(peer, n_col))

    def piece_peer(i):
        peer = lax.rem(piece + i, parts)
        return (lax.div(peer, pair), base_row + lax.rem(peer, pair), c)

    def far_peer(i):
        at = i - 1
        layer = lax.rem(g + 1 + lax.div(at, pair), n_gz)
        return (layer, base_row + lax.rem(at, pair), c)

    def greet(device):
        pl.semaphore_signal(barrier, inc=1, device_id=device, device_id_type=pl.DeviceIdType.MESH)

    each(group, lambda i: greet(group_peer(i)))
    each((n_gz - 1) * pair + 1, lambda i: greet(far_peer(i)))

    def send(src, dst, sems, at, device):
        pltpu.make_async_remote_copy(
            src_ref=src,
            dst_ref=dst,
            send_sem=sems.at[0, at],
            recv_sem=sems.at[1, at],
            device_id=device,
            device_id_type=pl.DeviceIdType.MESH,
        ).start()

    def wait_bytes(ref, sem):
        pltpu.make_async_copy(ref, ref, sem).wait()

    def pair_send(w):
        src, dst = sources[w]

        def step(i):
            to = (g, base_row + lax.rem(q + i, pair), c)
            send(src, dst.at[:, q], pair_sems, w - shared[0], to)

        each(pair, step)

    def ready(w):
        loads[w].wait()
        if pair > 1:
            ref = sources[w][1]
            wait_bytes(ref.at[:, pl.ds(0, pair - 1)], pair_sems.at[1, w - shared[0]])

    def weight(ref, at):
        return ref[at].reshape(pair * TILE, ref.shape[-1])

    def side_by_side(value):
        return jnp.concatenate([value[k] for k in range(pair)], axis=1)

    def in_order(block):
        order = [(t // n_col, t % n_col) for t in range(group)]
        return jnp.concatenate([block(x // pair * n_col + y, x % pair) for x, y in order], axis=1)

    def row_send(a):
        def step(i):
            other = lax.rem(r + i, n_row)
            send(upd.at[a, other], row_in.at[a, r], row_sems, a, (g, other, c))

        each(n_row, step)

    def row_finish(a):
        if n_row > 1:
            wait_bytes(row_in.at[a, pl.ds(0, n_row - 1)], row_sems.at[1, a])
        total = upd[a, r].astype(F32)
        for i in range(1, n_row):
            total = total + row_in[a, lax.rem(r + i, n_row)].astype(F32)
        row_sum[a] = total.astype(BF16)

    def gz_send(a):
        def step(i):
            other = lax.rem(g + i, n_gz)
            send(row_sum.at[a, other], gz_in.at[a, g], gz_sems, a, (other, r, c))

        each(n_gz, step)

    def gz_finish(a):
        if n_gz > 1:
            wait_bytes(gz_in.at[a, pl.ds(0, n_gz - 1)], gz_sems.at[1, a])
        total = row_sum[a, g].astype(F32)
        for i in range(1, n_gz):
            total = total + gz_in[a, lax.rem(g + i, n_gz)].astype(F32)
        gz_sum[a] = total.astype(BF16)

    def col_send(a):
        def step(i):
            other = lax.rem(c + i, n_col)
            send(gz_sum.at[a, other], col_in.at[a, c], col_sems, a, (g, r, other))

        each(n_col, step)

    def col_finish(a):
        if n_col > 1:
            wait_bytes(col_in.at[a, pl.ds(0, n_col - 1)], col_sems.at[1, a])
        total = gz_sum[a, c].astype(F32)
        for i in range(1, n_col):
            total = total + col_in[a, lax.rem(c + i, n_col)].astype(F32)
        return side_by_side(probe_t[a, :, piece] - total)

    def gather_send(step_at, value):
        for k in range(pair):
            rings[step_at, team, k] = value[:, k * TILE : (k + 1) * TILE]

        def step(i):
            own = rings.at[step_at, team]
            send(own, own, gather_sems, step_at, team_peer(i))

        each(teams, step)

    def gather_wait(step_at):
        if teams > 1:
            wait_bytes(rings.at[step_at, pl.ds(0, teams - 1)], gather_sems.at[1, step_at])
        return in_order(lambda at, k: rings[step_at, at, k])

    def solved_send(a, value):
        at = a * teams + team
        for k in range(pair):
            whole[piece, at, k] = value[:, k * TILE : (k + 1) * TILE]

        def step(i):
            own = whole.at[piece, at]
            send(own, own, gather_sems, 3 * levels - 1 + a, team_peer(i))

        each(teams, step)

    def solved_wait(a):
        if teams > 1:
            wait_bytes(
                whole.at[piece, pl.ds(a * teams, teams - 1)], gather_sems.at[1, 3 * levels - 1 + a]
            )
        return in_order(lambda at, k: whole[piece, a * teams + at, k])

    def whole_send(a):
        def step(i):
            own = whole.at[piece, pl.ds(a * teams, teams)]
            send(own, own, whole_sems, a, piece_peer(i))

        each(parts, step)

    def whole_wait(a):
        if parts > 1:
            wait_bytes(whole.at[pl.ds(0, parts - 1), pl.ds(a * teams, teams)], whole_sems.at[1, a])

    live = lax.broadcasted_iota(jnp.int32, (1, leaf_width), 1) < tiles_ref[0] * TILE
    loads[0].wait()
    masked = jnp.where(live, leaf_probe[0].astype(F32).T, 0.0).astype(BF16)
    loads[1].wait()
    solved = jnp.where(live, dot_t(masked, leaf_lower_inv[0]), 0.0).astype(BF16)
    solved_t[...] = solved
    pl.semaphore_wait(barrier, group - 1 + (n_gz - 1) * pair)
    for w in (3, 4, 5):
        pair_send(w)
    loads[2].wait()
    for j in range(couplings):
        rows = leaf_lower_panel[0, pl.ds(j * TILE, TILE), :]
        blocks_t[j] = dot_t(solved, rows).astype(BF16)
    blocks_t[couplings] = jnp.zeros(blocks_t.shape[1:], BF16)

    def spread(a):
        def place(t, carry):
            at = jnp.int32(couplings)
            for j in range(couplings):
                at = jnp.where(coupled_ref[0, j] == a * group + t, j, at)
            block = blocks_t[at]
            t_row, t_col = lax.div(t, n_col), lax.rem(t, n_col)
            first, place_in = lax.div(t_row, pair) * pair, lax.rem(t_row, pair)
            for k in range(parts):
                lines = block[k * part : (k + 1) * part]
                upd[a, first + k % pair, k // pair, t_col, place_in] = lines
            return carry

        lax.fori_loop(0, group, place, 0)

    spread(0)
    row_send(0)
    for a in range(1, levels):
        spread(a)
        row_send(a)
    row_finish(0)
    gz_send(0)
    ready(3)
    for a in range(levels):
        for k in range(pair):
            probe_t[a, k] = top_probe[a, k].astype(F32).T.reshape(probe_t.shape[2:])
    for a in range(1, levels):
        row_finish(a)
        gz_send(a)
    gz_finish(0)
    col_send(0)
    for w in (6, 7):
        pair_send(w)
    ready(4)
    ready(5)
    target = {0: col_finish(0)}

    forward = []
    for a in range(levels):
        gather_send(2 * a, target[a].astype(BF16))
        if a + 1 < levels:
            gz_finish(a + 1)
            col_send(a + 1)
        if a >= 1:
            for h in range(a + 1, levels):
                known = [l for l in range(levels) if l == a - 1]
                for l in known:
                    pending[h] = pending.get(h, 0.0) + dot_few(gathered[l], weight(top_lower_blocks, pair_index(h, l)))
        else:
            gathered = []
            pending = {}
        whole_rhs = gather_wait(2 * a)
        x = dot_few(whole_rhs, weight(top_lower_inv, a)).astype(BF16)
        forward.append(x)
        if a + 1 < levels:
            gather_send(2 * a + 1, x)
            base = col_finish(a + 1) - pending.get(a + 1, 0.0)
            gathered.append(gather_wait(2 * a + 1))
            target[a + 1] = base - dot_few(gathered[a], weight(top_lower_blocks, pair_index(a + 1, a)))

    ready(6)
    ready(7)
    rhs = forward[levels - 1]
    upper = {a: forward[a].astype(F32) for a in range(levels)}
    last = None
    for a in range(levels - 1, -1, -1):
        gather_send(forward_steps + a, rhs)
        if last is not None:
            whole_send(a + 1)
            for l in range(a):
                upper[l] = upper[l] - dot_few(last, weight(top_upper_blocks, pair_index(a + 1, l)))
        whole_rhs = gather_wait(forward_steps + a)
        solution_part = dot_few(whole_rhs, weight(top_upper_inv, a)).astype(BF16)
        solved_send(a, solution_part)
        if a == levels - 1:
            loads[8].wait()
            loads[9].wait()
        last = solved_wait(a)
        if a > 0:
            rhs = (upper[a - 1] - dot_few(last, weight(top_upper_blocks, pair_index(a, a - 1)))).astype(BF16)
    whole_send(0)

    def write_top(a):
        whole_wait(a)
        own = jnp.concatenate([whole[k, a * teams + team, q] for k in range(parts)], axis=0)
        top_out[a] = own.astype(F32).T

    for a in range(levels - 1, 0, -1):
        write_top(a)
    whole_wait(0)

    def where(tile):
        level, t = lax.div(tile, group), lax.rem(tile, group)
        x, y = lax.div(t, n_col), lax.rem(t, n_col)
        return level * teams + lax.div(x, pair) * n_col + y, lax.rem(x, pair)

    picked = jnp.concatenate(
        [
            jnp.concatenate([whole[(k, *where(coupled_ref[0, j]))] for k in range(parts)], axis=0)
            for j in range(couplings)
        ],
        axis=1,
    )
    back = solved_t[...].astype(F32) - dot_t(picked, leaf_upper_panel[0])
    back = jnp.where(live, back, 0.0).astype(BF16)
    answer = dot_t(leaf_upper_inv[0], back)
    live_rows = lax.broadcasted_iota(jnp.int32, (leaf_width, 1), 0) < tiles_ref[0] * TILE
    leaf_out[0] = jnp.where(live_rows, answer, 0.0)
    own = jnp.concatenate([whole[k, team, q] for k in range(parts)], axis=0)
    top_out[0] = own.astype(F32).T

    for a in range(levels):
        if n_row > 1:
            wait_bytes(row_in.at[a, pl.ds(0, n_row - 1)], row_sems.at[0, a])
        if n_gz > 1:
            wait_bytes(gz_in.at[a, pl.ds(0, n_gz - 1)], gz_sems.at[0, a])
        if parts > 1:
            wait_bytes(whole.at[pl.ds(0, parts - 1), pl.ds(a * teams, teams)], whole_sems.at[0, a])
        if n_col > 1:
            wait_bytes(col_in.at[a, pl.ds(0, n_col - 1)], col_sems.at[0, a])
    if teams > 1:
        for s in range(4 * levels - 1):
            wait_bytes(rings.at[0, pl.ds(0, teams - 1)], gather_sems.at[0, s])
    if pair > 1:
        for w in shared:
            ref = sources[w][1]
            wait_bytes(ref.at[:, pl.ds(0, pair - 1)], pair_sems.at[0, w - shared[0]])


def solution(mesh):
    n_gz, n_row, n_col = mesh.shape["gz"], mesh.shape["row"], mesh.shape["col"]
    group = n_row * n_col

    def body(
        leaf_probe,
        leaf_lower_inv,
        leaf_upper_inv,
        leaf_lower_panel,
        leaf_upper_panel,
        leaf_tiles,
        coupled,
        top_probe,
        top_lower_inv,
        top_lower_blocks,
        top_upper_inv,
        top_upper_blocks,
    ):
        leaves, leaf_width, columns = leaf_probe.shape
        levels, sep_rows, _ = top_probe.shape
        couplings = coupled.shape[1]
        weights = (top_lower_inv, top_lower_blocks, top_upper_inv, top_upper_blocks)
        small = sum(x.size * x.dtype.itemsize for x in weights) <= 12 * 2**20
        pair = 2 if small and n_row % 2 == 0 and columns % (n_gz * 32) == 0 else 1
        teams, parts = group // pair, n_gz * pair
        part = columns // parts
        assert leaves == 1 and sep_rows == TILE and part * parts == columns
        big = [
            leaf_probe,
            leaf_lower_inv,
            leaf_lower_panel,
            top_probe,
            top_lower_inv,
            top_lower_blocks,
            top_upper_inv,
            top_upper_blocks,
            leaf_upper_panel,
            leaf_upper_inv,
        ]
        sizes = (levels, n_gz, n_row, n_col, pair, part, couplings, leaf_width)
        dma = pltpu.SemaphoreType.DMA
        smem = pl.BlockSpec(memory_space=pltpu.SMEM)
        vmem = pl.BlockSpec(memory_space=pltpu.VMEM)
        anywhere = pl.BlockSpec(memory_space=pl.ANY)
        held = [
            (x.shape[0], pair, *x.shape[1:]) if i in range(3, 8) else x.shape
            for i, x in enumerate(big)
        ]
        scratch = [pltpu.VMEM(shape, x.dtype) for shape, x in zip(held, big)] + [
            pltpu.VMEM((columns, leaf_width), BF16),
            pltpu.VMEM((couplings + 1, columns, TILE), BF16),
            pltpu.VMEM((levels, pair, parts, part, TILE), F32),
            pltpu.VMEM((levels, n_row, n_gz, n_col, pair, part, TILE), BF16),
            pltpu.VMEM((levels, n_row, n_gz, n_col, pair, part, TILE), BF16),
            pltpu.VMEM((levels, n_gz, n_col, pair, part, TILE), BF16),
            pltpu.VMEM((levels, n_gz, n_col, pair, part, TILE), BF16),
            pltpu.VMEM((levels, n_col, pair, part, TILE), BF16),
            pltpu.VMEM((levels, n_col, pair, part, TILE), BF16),
            pltpu.VMEM((3 * levels - 1, teams, pair, part, TILE), BF16),
            pltpu.VMEM((parts, levels * teams, pair, part, TILE), BF16),
            dma((len(big),)),
            dma((2, 5)),
            dma((2, levels)),
            dma((2, levels)),
            dma((2, levels)),
            dma((2, 4 * levels - 1)),
            dma((2, levels)),
        ]
        return pl.pallas_call(
            functools.partial(kernel, sizes),
            out_shape=(
                jax.ShapeDtypeStruct(leaf_probe.shape, F32),
                jax.ShapeDtypeStruct(top_probe.shape, F32),
            ),
            in_specs=[smem, smem] + [anywhere] * len(big),
            out_specs=(vmem, vmem),
            scratch_shapes=scratch,
            compiler_params=pltpu.CompilerParams(
                collective_id=0, has_side_effects=True, vmem_limit_bytes=56 * 2**20
            ),
        )(leaf_tiles, coupled, *big)

    leaf3 = P(("gz", "row", "col"), None, None)
    top3 = P(None, ("row", "col"), None)
    return jax.shard_map(
        body,
        mesh=mesh,
        in_specs=(
            leaf3,
            leaf3,
            leaf3,
            leaf3,
            leaf3,
            P(("gz", "row", "col")),
            P(("gz", "row", "col"), None),
            top3,
            top3,
            top3,
            top3,
            top3,
        ),
        out_specs=(leaf3, top3),
        check_vma=False,
    )
```

```python
import functools

import jax
import jax.numpy as jnp
from jax import lax
from jax.experimental import pallas as pl
from jax.experimental.pallas import tpu as pltpu
from jax.sharding import PartitionSpec as P

TILE = 128
F32 = jnp.float32
BF16 = jnp.bfloat16


def pair_index(higher, lower):
    return higher * (higher - 1) // 2 + lower


def dot_t(left, right):
    return lax.dot_general(left, right, (((1,), (1,)), ((), ())), preferred_element_type=F32)


def kernel(
    sizes,
    tiles_ref,
    coupled_ref,
    leaf_probe_hbm,
    leaf_lower_inv_hbm,
    leaf_lower_panel_hbm,
    top_probe_hbm,
    top_lower_inv_hbm,
    top_lower_blocks_hbm,
    top_upper_inv_hbm,
    top_upper_blocks_hbm,
    leaf_upper_panel_hbm,
    leaf_upper_inv_hbm,
    leaf_out,
    top_out,
    leaf_probe,
    leaf_lower_inv,
    leaf_lower_panel,
    top_probe,
    top_lower_inv,
    top_lower_blocks,
    top_upper_inv,
    top_upper_blocks,
    leaf_upper_panel,
    leaf_upper_inv,
    solved_t,
    blocks_t,
    probe_t,
    upd,
    row_in,
    row_sum,
    gz_in,
    gz_sum,
    col_in,
    rings,
    whole,
    load_sem,
    row_sems,
    gz_sems,
    col_sems,
    gather_sems,
    whole_sems,
):
    levels, n_gz, n_row, n_col, part, couplings, leaf_width = sizes
    group = n_row * n_col
    g, r, c = lax.axis_index("gz"), lax.axis_index("row"), lax.axis_index("col")
    d = r * n_col + c
    forward_steps = 2 * levels - 1

    sources = [
        (leaf_probe_hbm, leaf_probe),
        (leaf_lower_inv_hbm, leaf_lower_inv),
        (leaf_lower_panel_hbm, leaf_lower_panel),
        (top_probe_hbm, top_probe),
        (top_lower_inv_hbm, top_lower_inv),
        (top_lower_blocks_hbm, top_lower_blocks),
        (top_upper_inv_hbm, top_upper_inv),
        (top_upper_blocks_hbm, top_upper_blocks),
        (leaf_upper_panel_hbm, leaf_upper_panel),
        (leaf_upper_inv_hbm, leaf_upper_inv),
    ]
    loads = [
        pltpu.make_async_copy(src, dst, load_sem.at[i]) for i, (src, dst) in enumerate(sources)
    ]
    for load in loads[:3]:
        load.start()

    def each(count, step):
        lax.fori_loop(1, count, lambda i, carry: (step(i), carry)[1], 0, unroll=count <= 8)

    barrier = pltpu.get_barrier_semaphore()

    def group_peer(i):
        peer = lax.rem(d + i, group)
        return (g, lax.div(peer, n_col), lax.rem(peer, n_col))

    def gz_peer(i):
        return (lax.rem(g + i, n_gz), r, c)

    def greet(device):
        pl.semaphore_signal(barrier, inc=1, device_id=device, device_id_type=pl.DeviceIdType.MESH)

    each(group, lambda i: greet(group_peer(i)))
    each(n_gz, lambda i: greet(gz_peer(i)))

    def send(src, dst, sems, at, device):
        pltpu.make_async_remote_copy(
            src_ref=src,
            dst_ref=dst,
            send_sem=sems.at[0, at],
            recv_sem=sems.at[1, at],
            device_id=device,
            device_id_type=pl.DeviceIdType.MESH,
        ).start()

    def wait_bytes(ref, sem):
        pltpu.make_async_copy(ref, ref, sem).wait()

    def row_send(a):
        def step(i):
            other = lax.rem(r + i, n_row)
            send(upd.at[a, other], row_in.at[a, r], row_sems, a, (g, other, c))

        each(n_row, step)

    def row_finish(a):
        if n_row > 1:
            wait_bytes(row_in.at[a, pl.ds(0, n_row - 1)], row_sems.at[1, a])
        total = upd[a, r].astype(F32)
        for i in range(1, n_row):
            total = total + row_in[a, lax.rem(r + i, n_row)].astype(F32)
        row_sum[a] = total.astype(BF16)

    def gz_send(a):
        def step(i):
            other = lax.rem(g + i, n_gz)
            send(row_sum.at[a, other], gz_in.at[a, g], gz_sems, a, (other, r, c))

        each(n_gz, step)

    def gz_finish(a):
        if n_gz > 1:
            wait_bytes(gz_in.at[a, pl.ds(0, n_gz - 1)], gz_sems.at[1, a])
        total = row_sum[a, g].astype(F32)
        for i in range(1, n_gz):
            total = total + gz_in[a, lax.rem(g + i, n_gz)].astype(F32)
        gz_sum[a] = total.astype(BF16)

    def col_send(a):
        def step(i):
            other = lax.rem(c + i, n_col)
            send(gz_sum.at[a, other], col_in.at[a, c], col_sems, a, (g, r, other))

        each(n_col, step)

    def col_finish(a):
        if n_col > 1:
            wait_bytes(col_in.at[a, pl.ds(0, n_col - 1)], col_sems.at[1, a])
        total = gz_sum[a, c].astype(F32)
        for i in range(1, n_col):
            total = total + col_in[a, lax.rem(c + i, n_col)].astype(F32)
        return probe_t[a, g] - total

    def gather_send(step_at, value):
        rings[step_at, d] = value

        def step(i):
            send(rings.at[step_at, d], rings.at[step_at, d], gather_sems, step_at, group_peer(i))

        each(group, step)

    def gather_wait(step_at):
        if group > 1:
            wait_bytes(rings.at[step_at, pl.ds(0, group - 1)], gather_sems.at[1, step_at])
        return jnp.concatenate([rings[step_at, i] for i in range(group)], axis=1)

    def solved_send(a, value):
        at = a * group + d
        whole[g, at] = value

        def step(i):
            send(whole.at[g, at], whole.at[g, at], gather_sems, 3 * levels - 1 + a, group_peer(i))

        each(group, step)

    def solved_wait(a):
        if group > 1:
            wait_bytes(
                whole.at[g, pl.ds(a * group, group - 1)], gather_sems.at[1, 3 * levels - 1 + a]
            )
        return jnp.concatenate([whole[g, a * group + i] for i in range(group)], axis=1)

    def whole_send(a):
        def step(i):
            at = pl.ds(a * group, group)
            send(whole.at[g, at], whole.at[g, at], whole_sems, a, gz_peer(i))

        each(n_gz, step)

    def whole_wait(a):
        if n_gz > 1:
            wait_bytes(whole.at[pl.ds(0, n_gz - 1), pl.ds(a * group, group)], whole_sems.at[1, a])

    live = lax.broadcasted_iota(jnp.int32, (1, leaf_width), 1) < tiles_ref[0] * TILE
    loads[0].wait()
    masked = jnp.where(live, leaf_probe[0].astype(F32).T, 0.0).astype(BF16)
    loads[1].wait()
    solved = jnp.where(live, dot_t(masked, leaf_lower_inv[0]), 0.0).astype(BF16)
    solved_t[...] = solved
    loads[2].wait()
    for load in loads[3:]:
        load.start()
    for j in range(couplings):
        rows = leaf_lower_panel[0, pl.ds(j * TILE, TILE), :]
        blocks_t[j] = dot_t(solved, rows).astype(BF16)
    blocks_t[couplings] = jnp.zeros(blocks_t.shape[1:], BF16)

    def spread(a):
        def place(t, carry):
            at = jnp.int32(couplings)
            for j in range(couplings):
                at = jnp.where(coupled_ref[0, j] == a * group + t, j, at)
            block = blocks_t[at]
            t_row, t_col = lax.div(t, n_col), lax.rem(t, n_col)
            for k in range(n_gz):
                upd[a, t_row, k, t_col] = block[k * part : (k + 1) * part]
            return carry

        lax.fori_loop(0, group, place, 0)

    spread(0)
    pl.semaphore_wait(barrier, group - 1 + n_gz - 1)
    row_send(0)
    if levels > 1:
        spread(1)
        row_send(1)
    row_finish(0)
    gz_send(0)
    for a in range(2, levels):
        spread(a)
        row_send(a)
    loads[3].wait()
    for a in range(levels):
        probe_t[a] = top_probe[a].astype(F32).T.reshape(probe_t.shape[1:])
    gz_finish(0)
    col_send(0)
    if levels > 1:
        row_finish(1)
        gz_send(1)
    loads[4].wait()
    loads[5].wait()
    target = {0: col_finish(0)}

    forward = []
    for a in range(levels):
        gather_send(2 * a, target[a].astype(BF16))
        if a + 1 < levels:
            gz_finish(a + 1)
            col_send(a + 1)
        if a + 2 < levels:
            row_finish(a + 2)
            gz_send(a + 2)
        if a >= 1:
            for h in range(a + 1, levels):
                known = [l for l in range(levels) if l == a - 1]
                for l in known:
                    pending[h] = pending.get(h, 0.0) + dot_t(gathered[l], top_lower_blocks[pair_index(h, l)])
        else:
            gathered = []
            pending = {}
        whole_rhs = gather_wait(2 * a)
        x = dot_t(whole_rhs, top_lower_inv[a]).astype(BF16)
        forward.append(x)
        if a + 1 < levels:
            gather_send(2 * a + 1, x)
            base = col_finish(a + 1) - pending.get(a + 1, 0.0)
            if a == 0:
                loads[6].wait()
                loads[7].wait()
            gathered.append(gather_wait(2 * a + 1))
            target[a + 1] = base - dot_t(gathered[a], top_lower_blocks[pair_index(a + 1, a)])

    rhs = forward[levels - 1]
    upper = {a: forward[a].astype(F32) for a in range(levels)}
    last = None
    for a in range(levels - 1, -1, -1):
        gather_send(forward_steps + a, rhs)
        if last is not None:
            whole_send(a + 1)
            for l in range(a):
                upper[l] = upper[l] - dot_t(last, top_upper_blocks[pair_index(a + 1, l)])
        whole_rhs = gather_wait(forward_steps + a)
        solution_part = dot_t(whole_rhs, top_upper_inv[a]).astype(BF16)
        solved_send(a, solution_part)
        if a == levels - 1:
            loads[8].wait()
            loads[9].wait()
        last = solved_wait(a)
        if a > 0:
            rhs = (upper[a - 1] - dot_t(last, top_upper_blocks[pair_index(a, a - 1)])).astype(BF16)
    whole_send(0)

    def write_top(a):
        whole_wait(a)
        own = jnp.concatenate([whole[k, a * group + d] for k in range(n_gz)], axis=0)
        top_out[a] = own.astype(F32).T.astype(BF16)

    for a in range(levels - 1, 0, -1):
        write_top(a)
    whole_wait(0)
    picked = jnp.concatenate(
        [
            jnp.concatenate([whole[k, coupled_ref[0, j]] for k in range(n_gz)], axis=0)
            for j in range(couplings)
        ],
        axis=1,
    )
    back = solved_t[...].astype(F32) - dot_t(picked, leaf_upper_panel[0])
    back = jnp.where(live, back, 0.0).astype(BF16)
    answer = dot_t(leaf_upper_inv[0], back)
    live_rows = lax.broadcasted_iota(jnp.int32, (leaf_width, 1), 0) < tiles_ref[0] * TILE
    leaf_out[0] = jnp.where(live_rows, answer, 0.0)
    own = jnp.concatenate([whole[k, d] for k in range(n_gz)], axis=0)
    top_out[0] = own.astype(F32).T.astype(BF16)

    for a in range(levels):
        if n_row > 1:
            wait_bytes(row_in.at[a, pl.ds(0, n_row - 1)], row_sems.at[0, a])
        if n_gz > 1:
            wait_bytes(gz_in.at[a, pl.ds(0, n_gz - 1)], gz_sems.at[0, a])
            wait_bytes(whole.at[pl.ds(0, n_gz - 1), pl.ds(a * group, group)], whole_sems.at[0, a])
        if n_col > 1:
            wait_bytes(col_in.at[a, pl.ds(0, n_col - 1)], col_sems.at[0, a])
    if group > 1:
        for s in range(4 * levels - 1):
            wait_bytes(rings.at[0, pl.ds(0, group - 1)], gather_sems.at[0, s])


def solution(mesh):
    n_gz, n_row, n_col = mesh.shape["gz"], mesh.shape["row"], mesh.shape["col"]
    group = n_row * n_col

    def body(
        leaf_probe,
        leaf_lower_inv,
        leaf_upper_inv,
        leaf_lower_panel,
        leaf_upper_panel,
        leaf_tiles,
        coupled,
        top_probe,
        top_lower_inv,
        top_lower_blocks,
        top_upper_inv,
        top_upper_blocks,
    ):
        leaves, leaf_width, columns = leaf_probe.shape
        levels, sep_rows, _ = top_probe.shape
        couplings = coupled.shape[1]
        part = columns // n_gz
        assert leaves == 1 and sep_rows == TILE and part * n_gz == columns
        big = [
            leaf_probe,
            leaf_lower_inv,
            leaf_lower_panel,
            top_probe,
            top_lower_inv,
            top_lower_blocks,
            top_upper_inv,
            top_upper_blocks,
            leaf_upper_panel,
            leaf_upper_inv,
        ]
        sizes = (levels, n_gz, n_row, n_col, part, couplings, leaf_width)
        dma = pltpu.SemaphoreType.DMA
        smem = pl.BlockSpec(memory_space=pltpu.SMEM)
        vmem = pl.BlockSpec(memory_space=pltpu.VMEM)
        anywhere = pl.BlockSpec(memory_space=pl.ANY)
        scratch = [pltpu.VMEM(x.shape, x.dtype) for x in big] + [
            pltpu.VMEM((columns, leaf_width), BF16),
            pltpu.VMEM((couplings + 1, columns, TILE), BF16),
            pltpu.VMEM((levels, n_gz, part, TILE), F32),
            pltpu.VMEM((levels, n_row, n_gz, n_col, part, TILE), BF16),
            pltpu.VMEM((levels, n_row, n_gz, n_col, part, TILE), BF16),
            pltpu.VMEM((levels, n_gz, n_col, part, TILE), BF16),
            pltpu.VMEM((levels, n_gz, n_col, part, TILE), BF16),
            pltpu.VMEM((levels, n_col, part, TILE), BF16),
            pltpu.VMEM((levels, n_col, part, TILE), BF16),
            pltpu.VMEM((3 * levels - 1, group, part, TILE), BF16),
            pltpu.VMEM((n_gz, levels * group, part, TILE), BF16),
            dma((len(big),)),
            dma((2, levels)),
            dma((2, levels)),
            dma((2, levels)),
            dma((2, 4 * levels - 1)),
            dma((2, levels)),
        ]
        leaf, top = pl.pallas_call(
            functools.partial(kernel, sizes),
            out_shape=(
                jax.ShapeDtypeStruct(leaf_probe.shape, F32),
                jax.ShapeDtypeStruct(top_probe.shape, BF16),
            ),
            in_specs=[smem, smem] + [anywhere] * len(big),
            out_specs=(vmem, vmem),
            scratch_shapes=scratch,
            compiler_params=pltpu.CompilerParams(
                collective_id=0, has_side_effects=True, vmem_limit_bytes=56 * 2**20
            ),
        )(leaf_tiles, coupled, *big)
        return leaf, top.astype(F32)

    leaf3 = P(("gz", "row", "col"), None, None)
    top3 = P(None, ("row", "col"), None)
    return jax.shard_map(
        body,
        mesh=mesh,
        in_specs=(
            leaf3,
            leaf3,
            leaf3,
            leaf3,
            leaf3,
            P(("gz", "row", "col")),
            P(("gz", "row", "col"), None),
            top3,
            top3,
            top3,
            top3,
            top3,
        ),
        out_specs=(leaf3, top3),
        check_vma=False,
    )
```
